128 devices in a mesh: prow: 8 (over y, x_lo), pcol: 16 (over z, x_hi, core).
Axes of the slice: x: 4 (x_hi: 2, x_lo: 2; x = x_hi * 2 + x_lo), y: 4, z: 4, core: 2. Of those that a mesh axis runs over, the one named last changes fastest.
Arguments:
- inverse_anc: bfloat16 [8192, 8192], P('prow', 'pcol')
- factor_one: bfloat16 [8192, 4096], P('prow', 'pcol'), may hold values from -0.75 to 0.75
- factor_zero: bfloat16 [8192, 8192], P('prow', 'pcol'), may hold values from -0.75 to 0.75
- factor_parent: bfloat16 [256, 8192], replicated, may hold values from -0.75 to 0.75
- dinv_one: float32 [256, 4096], P(None, 'pcol'), may hold values from -6 to 6
- dinv_zero: float32 [256, 8192], P(None, 'pcol'), may hold values from -6 to 6
- struct_one: int32 [16, 16], replicated, may hold values from 0 to 31, all different within a row
- select_zero: int32 [32, 8], replicated, may hold values from 0 to 15, all different within a row
- parent: int32 [32], replicated, may hold values from 0 to 15
Outputs:
- upper_one: bfloat16 [8192, 4096], P('prow', 'pcol')
- diag_one: float32 [256, 4096], P(None, 'pcol')
- upper_zero: bfloat16 [8192, 8192], P('prow', 'pcol')
- upper_parent: bfloat16 [256, 8192], P(None, 'pcol')
- diag_zero: float32 [256, 8192], P(None, 'pcol')
The draws below stay inside these ranges and needn't reach their ends.
Inputs may be any that keep to these rules, and one draw needn't show every extreme that they name: `struct_one`: each row names 16 different ancestor blocks. `select_zero`: each row names 8 different positions.
All inputs are finite; a program needn't handle non-finite values.
Results may differ from the reference program's by a relative error of at most 0.0034.
The reference program's roundings to bfloat16 on the way (of `diag_half` and `parent_link`) count: a program that leaves them out, or rounds other values in their place, can miss the bound.
Values may be sent and summed in bfloat16 or wider, within the bound.
No kernel may reach another device: no remote copies, remote signals or barrier semaphores. Data moves between devices by JAX's collectives and lax.ppermute only.
A program may use at most 192 MiB of HBM per device.

```python
import math
import jax
import jax.numpy as jnp
from jax import lax

B = 256
NA = 32
NP = 16
NC = 32
S1 = 16
S0 = 8


def draw_inverse_anc(key, part):
    key = jax.random.fold_in(key, 7)
    full_order = NA * B
    noise_base = jax.random.normal(key, (full_order, full_order), jnp.float32)
    spread = 1.6 / math.sqrt(S1 * B)
    return ((noise_base + noise_base.T) * spread + jnp.eye(full_order, dtype=jnp.float32)).astype(jnp.bfloat16)


def touch_ends(values, key, low, top_value):
    index_at = [jax.random.randint(jax.random.fold_in(key, axis), (), 0, length) for axis, length in enumerate(values.shape)]
    widest = values.shape.index(max(values.shape))
    next_to = index_at[:widest] + [(index_at[widest] + 1) % values.shape[widest]] + index_at[widest + 1:]
    return values.at[tuple(index_at)].set(low).at[tuple(next_to)].set(top_value)


def steps_of(key, shape, shards, low, largest):
    level, own = 1.0, jax.random.fold_in(key, 6)
    for position, parts in shards:
        heights = jnp.exp(jax.random.uniform(jax.random.fold_in(own, position), (parts,), jnp.float32, low / len(shards), largest / len(shards)))
        level = level * jnp.repeat(heights, shape[position] // parts).reshape([-1 if axis == position else 1 for axis in range(len(shape))])
    return level


def choose_distinct(key, rows, count, top, lift):
    sequence = jax.random.permutation(jax.random.fold_in(key, 1), count)
    pull = sequence
    for power in range(3):
        pull = pull * pull // count
    pull = pull * lift // count
    chance = jax.random.randint(jax.random.fold_in(key, 2), (rows, count), 0, 4096) + pull
    fixed_rows = jax.random.permutation(jax.random.fold_in(key, 3), rows)[jnp.arange(count) % rows]
    chance = jnp.where(jnp.arange(rows)[:, None] == fixed_rows[None, :], 1 << 14, chance)
    score = chance * count + jnp.arange(count)
    return lax.top_k(score.astype(jnp.int32), top)[1].astype(jnp.int32)


def scatter_about(stream_key, extent, scale, bound, split=(), held_as=jnp.bfloat16):
    array = scale * jax.random.normal(stream_key, extent, jnp.float32)
    if split:
        array = array * steps_of(stream_key, extent, split, -0.22, 0.18)
    return jnp.clip(array, -bound, bound).astype(held_as)


def setup_inputs(seed: int = 0) -> dict:
    key_list = jax.random.split(jax.random.key(seed), 10)
    inverse_anc = draw_inverse_anc(jax.random.fold_in(key_list[9], 71), 0)
    factor_one = scatter_about(key_list[1], (NA * B, NP * B), (S1 * B // 64) ** -0.5, 0.75, ((0, 8), (1, 16)))
    factor_zero = scatter_about(key_list[2], (NA * B, NC * B), (S1 * B // 64) ** -0.5, 0.75, ((0, 8), (1, 16)))
    factor_parent = scatter_about(key_list[3], (B, NC * B), (S1 * B // 64) ** -0.5, 0.75)
    dinv_one = scatter_about(key_list[4], (B, NP * B), 1.0, 6.0, ((1, 16),), jnp.float32)
    dinv_zero = scatter_about(key_list[5], (B, NC * B), 1.0, 6.0, ((1, 16),), jnp.float32)
    struct_one = choose_distinct(key_list[6], NP, NA, S1, 4096)
    select_zero = choose_distinct(key_list[7], NC, S1, S0, 0)
    parent = touch_ends(jax.random.randint(key_list[8], (NC,), 0, NP), jax.random.fold_in(key_list[8], 1), 0, NP - 1).astype(jnp.int32)
    return dict(inverse_anc=inverse_anc, factor_one=factor_one, factor_zero=factor_zero, factor_parent=factor_parent, dinv_one=dinv_one, dinv_zero=dinv_zero, struct_one=struct_one, select_zero=select_zero, parent=parent)


def block_mask(blocks, first_block, block_count, blk_width):
    wanted = first_block + jnp.arange(block_count, dtype=jnp.int32)
    matched = jnp.any(blocks[:, :, None] == wanted[None, None, :], axis=1)
    return jnp.repeat(jnp.repeat(matched.T, blk_width, axis=0), blk_width, axis=1)


def child_ancestors(struct_one, select_zero, parent):
    parent_rows = jnp.take(struct_one, parent, axis=0)
    return jnp.take_along_axis(parent_rows, select_zero, axis=1)


def block_products(left_side, right_side, group_count, blk_width):
    row_total = left_side.shape[0]
    left_blocks = left_side.astype(jnp.float32).reshape(row_total, group_count, blk_width)
    right_blocks = right_side.astype(jnp.float32).reshape(row_total, group_count, blk_width)
    return jnp.einsum("nik,nil->kil", left_blocks, right_blocks).reshape(blk_width, group_count * blk_width)


def reference(inverse_anc, factor_one, factor_zero, factor_parent, dinv_one, dinv_zero, struct_one, select_zero, parent):
    zero_half = jnp.zeros((), jnp.bfloat16)
    ancestors = child_ancestors(struct_one, select_zero, parent)
    mask_one = block_mask(struct_one, 0, NA, B)
    mask_zero = block_mask(ancestors, 0, NA, B)
    low_one = jnp.where(mask_one, factor_one, zero_half)
    low_zero = jnp.where(mask_zero, factor_zero, zero_half)
    first_term = jnp.dot(inverse_anc, low_one, preferred_element_type=jnp.float32)
    upper_one = jnp.where(mask_one, -first_term, 0.0).astype(jnp.bfloat16)
    diag_one = dinv_one - block_products(low_one, upper_one, NP, B)
    diag_half = diag_one.astype(jnp.bfloat16)
    owner_table = parent[None, :] == jnp.arange(NP, dtype=jnp.int32)[:, None]
    parent_link = jnp.where(owner_table[:, None, :, None], factor_parent.reshape(1, B, NC, B), zero_half).reshape(NP * B, NC * B)
    total_sum = jnp.dot(inverse_anc, low_zero, preferred_element_type=jnp.float32) + jnp.dot(upper_one, parent_link, preferred_element_type=jnp.float32)
    upper_zero = jnp.where(mask_zero, -total_sum, 0.0).astype(jnp.bfloat16)
    cross_full = jnp.dot(upper_one.T, low_zero, preferred_element_type=jnp.float32)
    picked = jnp.sum(jnp.where(owner_table[:, None, :, None], cross_full.reshape(NP, B, NC, B), 0.0), axis=0)
    diag_pick = jnp.sum(jnp.where(owner_table[None, :, :, None], diag_half.reshape(B, NP, 1, B), zero_half), axis=1)
    diag_term = jnp.einsum("icj,jcl->icl", diag_pick.astype(jnp.float32), factor_parent.astype(jnp.float32).reshape(B, NC, B))
    upper_parent = (-(picked + diag_term)).reshape(B, NC * B).astype(jnp.bfloat16)
    own_term = jnp.einsum("jck,jcl->kcl", factor_parent.astype(jnp.float32).reshape(B, NC, B), upper_parent.astype(jnp.float32).reshape(B, NC, B)).reshape(B, NC * B)
    diag_zero = dinv_zero - block_products(low_zero, upper_zero, NC, B) - own_term
    return upper_one, diag_one, upper_zero, upper_parent, diag_zero
```

```python
import jax
import jax.numpy as jnp
from jax import lax
from jax.experimental import pallas as pl
from jax.experimental.pallas import tpu as pltpu
from jax.sharding import PartitionSpec as P

MESH_AXES = ("prow", "pcol")
BF = jnp.bfloat16
F32 = jnp.float32
B = 256
LOC = 1024
PIECES = ((0, 0), (0, 1), (-1, 0), (1, 0), (-1, 1), (1, 1), (2, 0), (2, 1))
SLICES = ((0, 0), (0, 1), (-1, 0), (1, 0), (-1, 1), (1, 1), (2, 0), (2, 1))


def moves(dy=0, dxl=0, dz=0, dxh=0, dcore=0):
    pairs = []
    for y in range(4):
        for xl in range(2):
            for z in range(4):
                for xh in range(2):
                    for core in range(2):
                        src = (y * 2 + xl) * 16 + z * 4 + xh * 2 + core
                        dst = (((y + dy) % 4) * 2 + (xl ^ dxl)) * 16
                        dst += ((z + dz) % 4) * 4 + (xh ^ dxh) * 2 + (core ^ dcore)
                        pairs.append((src, dst))
    return pairs


X_HI = moves(dxh=1)
X_LO = moves(dxl=1)
Z_UP = moves(dz=1)
Z_DOWN = moves(dz=-1)
Y_UP = moves(dy=1)
Y_DOWN = moves(dy=-1)
SIBLING = moves(dcore=1)


def send(block, pairs):
    return lax.ppermute(block, MESH_AXES, pairs)


def ring_gather(own, swap, up, down):
    half = own.shape[0] // 2
    other = send(own, swap)
    below, above = send(own, up), send(own, down)
    other_below, other_above = send(other, up), send(other, down)
    far = (send(below[:half], up), send(above[half:], down))
    other_far = (send(other_below[:half], up), send(other_above[half:], down))
    return [(own,), (other,), (below,), (above,), (other_below,), (other_above,), far, other_far]


def dot(left, right):
    return jnp.dot(left, right, preferred_element_type=F32)


def dot_t(left, right):
    return lax.dot_general(left, right, (((0,), (0,)), ((), ())), preferred_element_type=F32)


VMEM = pl.BlockSpec(memory_space=pltpu.VMEM)
SMEM = pl.BlockSpec(memory_space=pltpu.SMEM)
ANY = pl.BlockSpec(memory_space=pl.ANY)


def call(body, out_shape, in_specs, scratch=(), limit=32):
    outs = [VMEM] * len(out_shape) if isinstance(out_shape, list) else VMEM
    return pl.pallas_call(
        body,
        out_shape=out_shape,
        in_specs=in_specs,
        out_specs=outs,
        scratch_shapes=list(scratch),
        compiler_params=pltpu.CompilerParams(vmem_limit_bytes=limit * 2**20),
    )


SLOT_AT = 0
SLICE_AT = 96
ROW_AT = 104
PAR_AT = 116


def halves(refs):
    if len(refs) == 1:
        return [(refs[0], 0), (refs[0], LOC // 2)]
    return [(refs[0], 0), (refs[1], 0)]


def level_one_body(counts, tab, *refs):
    inv_counts, low_counts = counts
    pos = 0
    inv_refs, low_refs = [], []
    for count in inv_counts:
        inv_refs.append(refs[pos : pos + count])
        pos += count
    for count in low_counts:
        low_refs.append(refs[pos : pos + count])
        pos += count
    own_ref, up_ref, part_ref, diag_ref, inv_s, low_s, acc, inv_sem, low_sem = refs[pos:]
    low_copies = []
    for q, group in enumerate(low_refs):
        at = pl.ds(pl.multiple_of(tab[SLICE_AT + q] * 32, 32), 32)
        span = 32 // len(group)
        for h, ref in enumerate(group):
            low_copies.append(
                pltpu.make_async_copy(
                    ref, low_s.at[pl.ds(h * span, span), at, :], low_sem.at[q, h]
                )
            )
    for copy in low_copies:
        copy.start()
    half = LOC // 2
    for q, group in enumerate(inv_refs):
        for hc in range(2):
            for hr, (ref, start) in enumerate(halves(group)):
                pltpu.make_async_copy(
                    ref.at[pl.ds(start, half), pl.ds(hc * B, B)],
                    inv_s.at[2 * q + hc, pl.ds(hr * half, half), :],
                    inv_sem.at[2 * q + hc, hr],
                ).start()
    acc[...] = jnp.zeros_like(acc)
    part_ref[...] = jnp.zeros_like(part_ref)
    diag_ref[...] = jnp.zeros_like(diag_ref)
    for copy in low_copies:
        copy.wait()

    def step(b, carry):
        for hr in range(2):
            view = inv_s.at[b, pl.ds(hr * half, half), :]
            pltpu.make_async_copy(view, view, inv_sem.at[b, hr]).wait()
        slot = tab[SLOT_AT + b]

        @pl.when(slot >= 0)
        def _():
            acc[...] += dot(inv_s[b], low_s[slot])

        for e in range(2):
            kid_slot = tab[SLOT_AT + 32 * (e + 1) + b]
            for rb in range(4):

                @pl.when((kid_slot >= 0) & (tab[ROW_AT + 4 * (e + 1) + rb] > 0))
                def _():
                    rows, cols = pl.ds(rb * B, B), pl.ds(e * B, B)
                    part_ref[rows, cols] += dot(inv_s[b, rows, :], low_s[kid_slot])

        return carry

    lax.fori_loop(0, 32, step, 0)
    for rb in range(4):
        rows = pl.ds(rb * B, B)
        up_ref[rows, :] = jnp.zeros((B, B), BF)

        @pl.when(tab[ROW_AT + rb] > 0)
        def _():
            up = (-acc[rows, :]).astype(BF)
            up_ref[rows, :] = up
            diag_ref[...] += dot_t(own_ref[rows, :], up)


def level_one(tab, inv_pieces, low_pieces, factor_one):
    counts = ([len(p) for p in inv_pieces], [len(p) for p in low_pieces])
    flat = [a for p in inv_pieces for a in p] + [a for p in low_pieces for a in p]

    def body(tab_ref, *refs):
        level_one_body(counts, tab_ref, *refs)

    return call(
        body,
        [
            jax.ShapeDtypeStruct((LOC, B), BF),
            jax.ShapeDtypeStruct((LOC, 2 * B), F32),
            jax.ShapeDtypeStruct((B, B), F32),
        ],
        [SMEM] + [ANY] * len(flat) + [VMEM],
        [
            pltpu.VMEM((32, LOC, B), BF),
            pltpu.VMEM((32, B, B), BF),
            pltpu.VMEM((LOC, B), F32),
            pltpu.SemaphoreType.DMA((32, 2)),
            pltpu.SemaphoreType.DMA((8, 2)),
        ],
        limit=48,
    )(tab, *flat, factor_one)


def pack_body(parent, spread, terms, dinv, out, diag):
    total = terms[0]
    for i in range(1, 8):
        total = total + terms[i]
    value = dinv[...] - total
    diag[...] = value
    half = value.astype(BF)
    for j in range(16):
        out[j, 0:64, :] = spread[parent[2 * j]]
        out[j, 64:128, :] = spread[parent[2 * j + 1]]
        out[j, 128:160, :] = half


def level_zero_body(tab, got, part, factor, link, up_ref, sums, both):
    both[...] = jnp.zeros_like(both)
    for e in range(2):
        cols = pl.ds(e * B, B)
        for rb in range(4):
            rows = pl.ds(rb * B, B)
            present = tab[ROW_AT + 4 * (e + 1) + rb] > 0

            @pl.when(jnp.logical_not(present))
            def _():
                up_ref[rows, cols] = jnp.zeros((B, B), BF)

            @pl.when(present)
            def _():
                above = got[4 * rb : 4 * rb + 4, e * 64 : e * 64 + 64, :].reshape(B, B)
                low = factor[rows, cols]
                total = part[rows, cols] + dot(above, link[:, cols])
                up = (-total).astype(BF)
                up_ref[rows, cols] = up
                both[0, :, cols] += dot_t(above, low)
                both[1, :, cols] += dot_t(low, up)

    for i in range(8):
        sums[i, 0:32, :] = both[0, i * 32 : i * 32 + 32, :]
        sums[i, 32:64, :] = both[1, i * 32 : i * 32 + 32, :]


def parent_body(tab, sums, got, link, out):
    total = sums[0]
    for i in range(1, 8):
        total = total + sums[i]
    ups = []
    for e in range(2):
        cols = slice(e * B, e * B + B)
        half = got[tab[PAR_AT + e], 128:160, :]
        ups.append((-(total[0:32, cols] + dot(half, link[:, cols]))).astype(BF))
    up = jnp.concatenate(ups, axis=1)
    high = total[32:64].astype(BF)
    rest = (total[32:64] - high.astype(F32)).astype(BF)
    for i in range(8):
        out[i, 0:32, :] = up
        out[i, 32:64, :] = high
        out[i, 64:96, :] = rest


def last_body(got, dinv, link, up_ref, diag_ref):
    for i in range(8):
        rows = pl.ds(i * 32, 32)
        up_ref[rows, :] = got[i, 0:32, :]
        diag_ref[rows, :] = dinv[rows, :] - (
            got[i, 32:64, :].astype(F32) + got[i, 64:96, :].astype(F32)
        )
    for e in range(2):
        cols = pl.ds(e * B, B)
        diag_ref[:, cols] -= dot_t(link[:, cols], up_ref[:, cols])


def position_of(blocks, offset):
    places = jnp.where(
        blocks[:, None] == jnp.arange(32, dtype=jnp.int32)[None, :],
        jnp.arange(blocks.shape[0], dtype=jnp.int32)[:, None] + offset,
        -1,
    )
    return jnp.max(places, axis=0)


def tables(struct_one, select_zero, parent, row, col):
    own = lax.dynamic_slice_in_dim(struct_one, col, 1, 0)[0]
    parents = lax.dynamic_slice_in_dim(parent, 2 * col, 2, 0)
    picks = lax.dynamic_slice_in_dim(select_zero, 2 * col, 2, 0)
    kids = jnp.take_along_axis(jnp.take(struct_one, parents, axis=0), picks, axis=1)
    z, xh, core = col // 4, (col // 2) % 2, col % 2
    y, xl = row // 2, row % 2
    columns = []
    for dcore in range(2):
        for dz, dxh in PIECES:
            columns.append(((z + dz) % 4) * 4 + (xh ^ dxh) * 2 + (core ^ dcore))
    order = jnp.stack([2 * c + h for c in columns for h in range(2)])
    slots, rows = [], []
    for e, blocks in enumerate((own, kids[0], kids[1])):
        at = position_of(blocks, (0, 16, 24)[e])
        slots.append(jnp.take(at, order))
        rows.append(lax.dynamic_slice_in_dim(at, 4 * row, 4, 0) >= 0)
    slices = jnp.stack([((y + dy) % 4) * 2 + (xl ^ dxl) for dy, dxl in SLICES])
    tab = jnp.concatenate(
        slots + [slices] + [r.astype(jnp.int32) for r in rows] + [parents]
    ).astype(jnp.int32)
    chosen = jnp.concatenate([(b // 4) * 12 + e * 4 + b % 4 for e, b in enumerate((own, kids[0], kids[1]))])
    return tab, chosen


def shards(
    inverse_anc,
    factor_one,
    factor_zero,
    factor_parent,
    dinv_one,
    dinv_zero,
    struct_one,
    select_zero,
    parent,
):
    row = lax.axis_index("prow")
    col = lax.axis_index("pcol")
    tab, chosen = tables(struct_one, select_zero, parent, row, col)
    link = lax.dynamic_slice_in_dim(factor_parent, col * 2 * B, 2 * B, 1)
    dinv_rows = lax.dynamic_slice_in_dim(dinv_one, row * 32, 32, 0)

    pieces = ring_gather(inverse_anc, X_HI, Z_UP, Z_DOWN)
    pieces = pieces + [tuple(send(a, SIBLING) for a in p) for p in pieces]

    spread_low = jnp.concatenate(
        [
            factor_one.reshape(4, 8, 1, 32, B).transpose(1, 2, 0, 3, 4),
            factor_zero.reshape(4, 8, 32, 2, B).transpose(1, 3, 0, 2, 4),
        ],
        axis=1,
    )
    spread_low = lax.all_to_all(spread_low, "prow", 0, 0)
    mine = jnp.take(spread_low.reshape(96, 32, B), chosen, axis=0)
    low_pieces = ring_gather(mine, X_LO, Y_UP, Y_DOWN)

    upper_one, part, diag_part = level_one(tab, pieces, low_pieces, factor_one)

    spread = lax.all_to_all(upper_one.reshape(16, 64, B), "pcol", 0, 0)
    terms = lax.all_to_all(diag_part.reshape(8, 32, B), "prow", 0, 0)
    packed, diag_rows = call(
        pack_body,
        [jax.ShapeDtypeStruct((16, 160, B), BF), jax.ShapeDtypeStruct((32, B), F32)],
        [SMEM, VMEM, VMEM, VMEM],
    )(parent, spread, terms, dinv_rows)
    diag_one = lax.all_gather(diag_rows, "prow", axis=0, tiled=True)
    got = lax.all_to_all(packed, "pcol", 0, 0)
    upper_zero, sums = call(
        level_zero_body,
        [jax.ShapeDtypeStruct((LOC, 2 * B), BF), jax.ShapeDtypeStruct((8, 64, 2 * B), F32)],
        [SMEM, VMEM, VMEM, VMEM, VMEM],
        [pltpu.VMEM((2, B, 2 * B), F32)],
    )(tab, got, part, factor_zero, link)
    sums = lax.all_to_all(sums, "prow", 0, 0)
    rows_out = call(
        parent_body,
        jax.ShapeDtypeStruct((8, 96, 2 * B), BF),
        [SMEM, VMEM, VMEM, VMEM],
    )(tab, sums, got, link)
    rows_in = lax.all_to_all(rows_out, "prow", 0, 0)
    upper_parent, diag_zero = call(
        last_body,
        [jax.ShapeDtypeStruct((B, 2 * B), BF), jax.ShapeDtypeStruct((B, 2 * B), F32)],
        [VMEM, VMEM, VMEM],
    )(rows_in, dinv_zero, link)
    return upper_one, diag_one, upper_zero, upper_parent, diag_zero


def solution(mesh):
    in_specs = (
        P("prow", "pcol"),
        P("prow", "pcol"),
        P("prow", "pcol"),
        P(),
        P(None, "pcol"),
        P(None, "pcol"),
        P(),
        P(),
        P(),
    )
    out_specs = (
        P("prow", "pcol"),
        P(None, "pcol"),
        P("prow", "pcol"),
        P(None, "pcol"),
        P(None, "pcol"),
    )
    return jax.shard_map(shards, mesh=mesh, in_specs=in_specs, out_specs=out_specs, check_vma=False)
```

```python
import jax
import jax.numpy as jnp
from jax import lax
from jax.experimental import pallas as pl
from jax.experimental.pallas import tpu as pltpu
from jax.sharding import PartitionSpec as P

MESH_AXES = ("prow", "pcol")
BF = jnp.bfloat16
F32 = jnp.float32
B = 256
LOC = 1024
def moves(dy=0, dxl=0, dz=0, dxh=0, dcore=0):
    pairs = []
    for y in range(4):
        for xl in range(2):
            for z in range(4):
                for xh in range(2):
                    for core in range(2):
                        src = (y * 2 + xl) * 16 + z * 4 + xh * 2 + core
                        dst = (((y + dy) % 4) * 2 + (xl ^ dxl)) * 16
                        dst += ((z + dz) % 4) * 4 + (xh ^ dxh) * 2 + (core ^ dcore)
                        pairs.append((src, dst))
    return pairs


X_HI = moves(dxh=1)
X_LO = moves(dxl=1)
Z_UP = moves(dz=1)
Z_DOWN = moves(dz=-1)
Y_UP = moves(dy=1)
Y_DOWN = moves(dy=-1)
SIBLING = moves(dcore=1)


def send(block, pairs):
    return lax.ppermute(block, MESH_AXES, pairs)


def dot(left, right):
    return jnp.dot(left, right, preferred_element_type=F32)


def dot_t(left, right):
    return lax.dot_general(left, right, (((0,), (0,)), ((), ())), preferred_element_type=F32)


VMEM = pl.BlockSpec(memory_space=pltpu.VMEM)
SMEM = pl.BlockSpec(memory_space=pltpu.SMEM)
HBM = pl.BlockSpec(memory_space=pltpu.HBM)


def call(body, out_shape, in_specs, scratch=(), limit=32, flops=0, moved=0):
    outs = [VMEM] * len(out_shape) if isinstance(out_shape, list) else VMEM
    cost = pl.CostEstimate(flops=flops, bytes_accessed=moved, transcendentals=0)
    return pl.pallas_call(
        body,
        cost_estimate=cost if flops else None,
        out_shape=out_shape,
        in_specs=in_specs,
        out_specs=outs,
        scratch_shapes=list(scratch),
        compiler_params=pltpu.CompilerParams(vmem_limit_bytes=limit * 2**20),
    )


POS_AT = 0
SLICE_AT = 32
ROW_AT = 40
PAR_AT = 52
PICK_AT = 54
TABLE = 86


def table_body(place, struct, select, parent, tab):
    row, col = place[0], place[1]
    z, xh, core = col // 4, (col // 2) % 2, col % 2
    y, xl = row // 2, row % 2
    parents = [parent[2 * col], parent[2 * col + 1]]
    blocks = [struct[col, n] for n in range(16)]
    for e in range(2):
        tab[PAR_AT + e] = parents[e]
        blocks += [struct[parents[e], select[2 * col + e, n]] for n in range(8)]
    for n, block in enumerate(blocks):
        home = block // 2
        piece = ((home // 4) + 4 - z) % 4
        piece += 4 * (((home // 2) % 2 + xh) % 2) + 8 * ((home % 2 + core) % 2)
        tab[POS_AT + n] = 2 * piece + block % 2
        group = 0 if n < 16 else (1 if n < 24 else 2)
        tab[PICK_AT + n] = (block // 4) * 12 + group * 4 + block % 4
    for group, (low, high) in enumerate(((0, 16), (16, 24), (24, 32))):
        for rb in range(4):
            found = jnp.int32(0)
            for n in range(low, high):
                found = found + (blocks[n] == 4 * row + rb).astype(jnp.int32)
            tab[ROW_AT + 4 * group + rb] = found
    for k in range(8):
        tab[SLICE_AT + k] = ((y + k % 4) % 4) * 2 + (xl + k // 4) % 2


def build_body(one, zero, out):
    for i in range(8):
        for t in range(4):
            rows = pl.ds(t * B + i * 32, 32)
            out[i, 0, t] = one[rows, :]
            out[i, 1, t] = zero[rows, 0:B]
            out[i, 2, t] = zero[rows, B : 2 * B]


def pick_body(tab, spread, out):
    for n in range(32):
        out[n] = spread[tab[PICK_AT + n]]


def load(tab, inv_refs, low_refs, first, count, inv_s, low_s, inv_sem, low_sem):
    copies = []
    for q, ref in enumerate(low_refs):
        at = pl.ds(pl.multiple_of(tab[SLICE_AT + q] * 32, 32), 32)
        copies.append(
            pltpu.make_async_copy(
                ref.at[pl.ds(first, count)], low_s.at[:, at, :], low_sem.at[q]
            )
        )
    for q, ref in enumerate(inv_refs):
        for h in range(2):
            copies.append(
                pltpu.make_async_copy(
                    ref.at[:, pl.ds(h * B, B)], inv_s.at[2 * q + h], inv_sem.at[2 * q + h]
                )
            )
    for copy in copies:
        copy.start()
    return copies


def product(tab, inv_s, low_s, first, n):
    total = dot(inv_s[tab[POS_AT + first + n]], low_s[n])
    for j in range(1, 4):
        total += dot(inv_s[tab[POS_AT + first + n + j]], low_s[n + j])
    return total


def kids_body(tab, *refs):
    inv_refs, low_refs = refs[:16], refs[16:24]
    part_ref, inv_s, low_s, inv_sem, low_sem = refs[24:]
    copies = load(tab, inv_refs, low_refs, 16, 16, inv_s, low_s, inv_sem, low_sem)
    part_ref[...] = jnp.zeros_like(part_ref)
    for copy in copies:
        copy.wait()

    def step(n, carry):
        cols = pl.ds(pl.multiple_of((n // 2) * B, B), B)
        part_ref[:, cols] += product(tab, inv_s, low_s, 16, 4 * n)
        return carry

    lax.fori_loop(0, 4, step, 0)


def level_one_body(tab, *refs):
    inv_refs, low_refs = refs[:16], refs[16:24]
    own_ref, up_ref = refs[24:26]
    diag_refs = refs[26:34]
    inv_s, low_s, acc, diag, inv_sem, low_sem = refs[34:]
    copies = load(tab, inv_refs, low_refs, 0, 16, inv_s, low_s, inv_sem, low_sem)
    acc[...] = jnp.zeros_like(acc)
    diag[...] = jnp.zeros_like(diag)
    for copy in copies:
        copy.wait()

    def own_step(n, carry):
        acc[...] += product(tab, inv_s, low_s, 0, 4 * n)
        return carry

    lax.fori_loop(0, 4, own_step, 0)
    for rb in range(4):
        rows = pl.ds(rb * B, B)
        up_ref[rows, :] = jnp.zeros((B, B), BF)

        @pl.when(tab[ROW_AT + rb] > 0)
        def _():
            up = (-acc[rows, :]).astype(BF)
            up_ref[rows, :] = up
            diag[...] += dot_t(own_ref[rows, :], up)

    for k in range(8):
        at = pl.ds(pl.multiple_of(tab[SLICE_AT + k] * 32, 32), 32)
        diag_refs[k][...] = diag[at, :]


def level_one(tab, inv_pieces, low_pieces, factor_one):
    return call(
        level_one_body,
        [
            jax.ShapeDtypeStruct((LOC, B), BF),
        ]
        + [jax.ShapeDtypeStruct((32, B), F32)] * 8,
        [SMEM] + [HBM] * 24 + [VMEM],
        [
            pltpu.VMEM((32, LOC, B), BF),
            pltpu.VMEM((16, B, B), BF),
            pltpu.VMEM((LOC, B), F32),
            pltpu.VMEM((B, B), F32),
            pltpu.SemaphoreType.DMA((32,)),
            pltpu.SemaphoreType.DMA((8,)),
        ],
        limit=30,
    )(tab, *inv_pieces, *low_pieces, factor_one)


def kids(tab, inv_pieces, low_pieces):
    return call(
        kids_body,
        jax.ShapeDtypeStruct((LOC, 2 * B), F32),
        [SMEM] + [HBM] * 24,
        [
            pltpu.VMEM((32, LOC, B), BF),
            pltpu.VMEM((16, B, B), BF),
            pltpu.SemaphoreType.DMA((32,)),
            pltpu.SemaphoreType.DMA((8,)),
        ],
        limit=56,
        flops=2 * LOC * 16 * B * B,
        moved=24 * 2**20,
    )(tab, *inv_pieces, *low_pieces)


def pack_body(parent, spread, dinv, *refs):
    terms, out, diag = refs[:8], refs[8], refs[9]
    total = terms[0][...]
    for i in range(1, 8):
        total = total + terms[i][...]
    value = dinv[...] - total
    diag[...] = value
    half = value.astype(BF)
    for j in range(16):
        out[j, 0:64, :] = spread[parent[2 * j]]
        out[j, 64:128, :] = spread[parent[2 * j + 1]]
        out[j, 128:160, :] = half


def level_zero_body(tab, got, part, factor, link, up_ref, sums, both):
    both[...] = jnp.zeros_like(both)
    for e in range(2):
        cols = pl.ds(e * B, B)
        for rb in range(4):
            rows = pl.ds(rb * B, B)
            present = tab[ROW_AT + 4 * (e + 1) + rb] > 0

            @pl.when(jnp.logical_not(present))
            def _():
                up_ref[rows, cols] = jnp.zeros((B, B), BF)

            @pl.when(present)
            def _():
                above = got[4 * rb : 4 * rb + 4, e * 64 : e * 64 + 64, :].reshape(B, B)
                low = factor[rows, cols]
                total = part[rows, cols] + dot(above, link[:, cols])
                up = (-total).astype(BF)
                up_ref[rows, cols] = up
                both[0, :, cols] += dot_t(above, low)
                both[1, :, cols] += dot_t(low, up)

    for i in range(8):
        sums[i, 0:32, :] = both[0, i * 32 : i * 32 + 32, :]
        sums[i, 32:64, :] = both[1, i * 32 : i * 32 + 32, :]


def parent_body(tab, sums, got, link, diag, out):
    total = sums[0]
    for i in range(1, 8):
        total = total + sums[i]
    ups = []
    for e in range(2):
        cols = slice(e * B, e * B + B)
        half = got[tab[PAR_AT + e], 128:160, :]
        ups.append((-(total[0:32, cols] + dot(half, link[:, cols]))).astype(BF))
    up = jnp.concatenate(ups, axis=1)
    high = total[32:64].astype(BF)
    rest = (total[32:64] - high.astype(F32)).astype(BF)
    one_high = diag[...].astype(BF)
    one_rest = (diag[...] - one_high.astype(F32)).astype(BF)
    one = jnp.concatenate([one_high, one_rest], axis=1)
    for i in range(8):
        out[i, 96:128, :] = one
        out[i, 0:32, :] = up
        out[i, 32:64, :] = high
        out[i, 64:96, :] = rest


def last_body(got, dinv, link, up_ref, diag_ref, one_ref):
    for i in range(8):
        rows = pl.ds(i * 32, 32)
        up_ref[rows, :] = got[i, 0:32, :]
        one_ref[rows, :] = got[i, 96:128, 0:B].astype(F32) + got[i, 96:128, B : 2 * B].astype(F32)
        diag_ref[rows, :] = dinv[rows, :] - (
            got[i, 32:64, :].astype(F32) + got[i, 64:96, :].astype(F32)
        )
    for e in range(2):
        cols = pl.ds(e * B, B)
        diag_ref[:, cols] -= dot_t(link[:, cols], up_ref[:, cols])


def shards(
    inverse_anc,
    factor_one,
    factor_zero,
    factor_parent,
    dinv_one,
    dinv_zero,
    struct_one,
    select_zero,
    parent,
):
    row = lax.axis_index("prow")
    col = lax.axis_index("pcol")
    tab = pl.pallas_call(
        table_body,
        out_shape=jax.ShapeDtypeStruct((TABLE,), jnp.int32),
        in_specs=[SMEM] * 4,
        out_specs=SMEM,
    )(jnp.stack([row, col]).astype(jnp.int32), struct_one, select_zero, parent)
    link = lax.dynamic_slice_in_dim(factor_parent, col * 2 * B, 2 * B, 1)
    dinv_rows = lax.dynamic_slice_in_dim(dinv_one, row * 32, 32, 0)

    barrier = lax.optimization_barrier
    below, above = send(inverse_anc, Z_UP), send(inverse_anc, Z_DOWN)
    other = send(inverse_anc, X_HI)
    spread_low = call(
        build_body, jax.ShapeDtypeStruct((8, 3, 4, 32, B), BF), [VMEM, VMEM]
    )(factor_one, factor_zero)
    spread_low = lax.all_to_all(spread_low, "prow", 0, 0)

    own, below, above = barrier((inverse_anc, below, above))
    far = send(below, Z_UP)
    sib_own, sib_below, sib_above = send(own, SIBLING), send(below, SIBLING), send(above, SIBLING)

    spread_low, other, sib_own, sib_below, sib_above = barrier(
        (spread_low, other, sib_own, sib_below, sib_above)
    )
    other_above, other_below = send(other, Z_DOWN), send(other, Z_UP)
    mine = call(pick_body, jax.ShapeDtypeStruct((32, 32, B), BF), [SMEM, VMEM])(
        tab, spread_low.reshape(96, 32, B)
    )
    low_below, low_above = send(mine, Y_UP), send(mine, Y_DOWN)
    low_other = send(mine, X_LO)
    other_far = send(far, X_HI)
    sib_far, sib_other = send(far, SIBLING), send(other, SIBLING)
    low_far = send(low_below, Y_UP)
    low_other_above, low_other_below = send(low_other, Y_DOWN), send(low_other, Y_UP)
    low_other_far = send(low_other_above, Y_DOWN)
    sib_other_below, sib_other_above = send(other_below, SIBLING), send(other_above, SIBLING)
    sib_other_far = send(other_far, SIBLING)
    pieces = [own, above, far, below, other, other_above, other_far, other_below]
    pieces += [sib_own, sib_above, sib_far, sib_below]
    pieces += [sib_other, sib_other_above, sib_other_far, sib_other_below]
    low_pieces = [mine, low_above, low_far, low_below]
    low_pieces += [low_other, low_other_above, low_other_far, low_other_below]

    upper_one, *diag_parts = level_one(tab, pieces, low_pieces, factor_one)
    part = kids(tab, pieces, low_pieces)

    spread = lax.all_to_all(upper_one.reshape(16, 64, B), "pcol", 0, 0)
    terms = [diag_parts[0]]
    for k in range(1, 8):
        terms.append(send(diag_parts[k], moves(dy=k % 4, dxl=k // 4)))
    packed, diag_rows = call(
        pack_body,
        [jax.ShapeDtypeStruct((16, 160, B), BF), jax.ShapeDtypeStruct((32, B), F32)],
        [SMEM] + [VMEM] * 10,
    )(parent, spread, dinv_rows, *terms)
    got = lax.all_to_all(packed, "pcol", 0, 0)
    upper_zero, sums = call(
        level_zero_body,
        [jax.ShapeDtypeStruct((LOC, 2 * B), BF), jax.ShapeDtypeStruct((8, 64, 2 * B), F32)],
        [SMEM, VMEM, VMEM, VMEM, VMEM],
        [pltpu.VMEM((2, B, 2 * B), F32)],
    )(tab, got, part, factor_zero, link)
    sums = lax.all_to_all(sums, "prow", 0, 0)
    rows_out = call(
        parent_body,
        jax.ShapeDtypeStruct((8, 128, 2 * B), BF),
        [SMEM, VMEM, VMEM, VMEM, VMEM],
    )(tab, sums, got, link, diag_rows)
    rows_in = lax.all_to_all(rows_out, "prow", 0, 0)
    upper_parent, diag_zero, diag_one = call(
        last_body,
        [
            jax.ShapeDtypeStruct((B, 2 * B), BF),
            jax.ShapeDtypeStruct((B, 2 * B), F32),
            jax.ShapeDtypeStruct((B, B), F32),
        ],
        [VMEM, VMEM, VMEM],
    )(rows_in, dinv_zero, link)
    return upper_one, diag_one, upper_zero, upper_parent, diag_zero


def solution(mesh):
    in_specs = (
        P("prow", "pcol"),
        P("prow", "pcol"),
        P("prow", "pcol"),
        P(),
        P(None, "pcol"),
        P(None, "pcol"),
        P(),
        P(),
        P(),
    )
    out_specs = (
        P("prow", "pcol"),
        P(None, "pcol"),
        P("prow", "pcol"),
        P(None, "pcol"),
        P(None, "pcol"),
    )
    return jax.shard_map(shards, mesh=mesh, in_specs=in_specs, out_specs=out_specs, check_vma=False)
```

```python
import jax
import jax.numpy as jnp
from jax import lax
from jax.experimental import pallas as pl
from jax.experimental.pallas import tpu as pltpu
from jax.sharding import PartitionSpec as P

MESH_AXES = ("prow", "pcol")
BF = jnp.bfloat16
F32 = jnp.float32
B = 256
LOC = 1024
def moves(dy=0, dxl=0, dz=0, dxh=0, dcore=0):
    pairs = []
    for y in range(4):
        for xl in range(2):
            for z in range(4):
                for xh in range(2):
                    for core in range(2):
                        src = (y * 2 + xl) * 16 + z * 4 + xh * 2 + core
                        dst = (((y + dy) % 4) * 2 + (xl ^ dxl)) * 16
                        dst += ((z + dz) % 4) * 4 + (xh ^ dxh) * 2 + (core ^ dcore)
                        pairs.append((src, dst))
    return pairs


X_HI = moves(dxh=1)
X_LO = moves(dxl=1)
Z_UP = moves(dz=1)
Z_DOWN = moves(dz=-1)
Y_UP = moves(dy=1)
Y_DOWN = moves(dy=-1)
SIBLING = moves(dcore=1)


def send(block, pairs):
    return lax.ppermute(block, MESH_AXES, pairs)


def dot(left, right):
    return jnp.dot(left, right, preferred_element_type=F32)


def dot_t(left, right):
    return lax.dot_general(left, right, (((0,), (0,)), ((), ())), preferred_element_type=F32)


VMEM = pl.BlockSpec(memory_space=pltpu.VMEM)
SMEM = pl.BlockSpec(memory_space=pltpu.SMEM)
HBM = pl.BlockSpec(memory_space=pltpu.HBM)


def call(body, out_shape, in_specs, scratch=(), limit=32, flops=0, moved=0):
    outs = [VMEM] * len(out_shape) if isinstance(out_shape, list) else VMEM
    cost = pl.CostEstimate(flops=flops, bytes_accessed=moved, transcendentals=0)
    return pl.pallas_call(
        body,
        cost_estimate=cost if flops else None,
        out_shape=out_shape,
        in_specs=in_specs,
        out_specs=outs,
        scratch_shapes=list(scratch),
        compiler_params=pltpu.CompilerParams(vmem_limit_bytes=limit * 2**20),
    )


POS_AT = 0
SLICE_AT = 64
ROW_AT = 72
PAR_AT = 88
PICK_AT = 90
CORE_AT = 122
TABLE = 123
LISTS = ((0, 16), (16, 32), (32, 40), (40, 48), (48, 56), (56, 64))


def table_body(place, struct, select, parent, tab):
    row, col = place[0], place[1]
    core = col & 1
    y, xl = row >> 1, row & 1
    sib = col ^ 1
    blocks = [struct[col, n] for n in range(16)] + [struct[sib, n] for n in range(16)]
    for where in (col, sib):
        for e in range(2):
            kid = 2 * where + e
            home = parent[kid]
            blocks += [struct[home, select[kid, n]] for n in range(8)]
    for e in range(2):
        tab[PAR_AT + e] = parent[2 * col + e]
    for n, block in enumerate(blocks):
        home = block >> 1
        apart = ((home >> 2) - (col >> 2)) & 3
        other = (home ^ col) & 3
        tab[POS_AT + n] = 4 * apart + 16 * (other >> 1) + 2 * (other & 1) + (block & 1)
    for n in range(32):
        index = n if n < 16 else n + 16
        group = 0 if n < 16 else (1 if n < 24 else 2)
        block = blocks[index]
        tab[PICK_AT + n] = (block >> 2) * 12 + group * 4 + (block & 3)
    for n in range(ROW_AT, ROW_AT + 16):
        tab[n] = 0
    for group in range(4):
        low, high = LISTS[group]
        for n in range(low, high):
            block = blocks[n]

            @pl.when((block >> 2) == row)
            def _():
                tab[ROW_AT + 4 * group + (block & 3)] = 1

    for k in range(8):
        tab[SLICE_AT + k] = ((y + k) & 3) * 2 + (xl ^ (k // 4))
    tab[CORE_AT] = core


def build_body(one, zero, out):
    for i in range(8):
        for t in range(4):
            rows = pl.ds(t * B + i * 32, 32)
            out[i, 0, t] = one[rows, :]
            out[i, 1, t] = zero[rows, 0:B]
            out[i, 2, t] = zero[rows, B : 2 * B]


def pick_body(tab, spread, out):
    for n in range(32):
        out[n] = spread[tab[PICK_AT + n]]


HALF = LOC // 2


def collect_body(tab, *refs):
    outs, sem = refs[8:10], refs[10]
    copies = []
    for q in range(8):
        at = pl.ds(pl.multiple_of(tab[SLICE_AT + q] * 32, 32), 32)
        for e in range(2):
            copies.append(
                pltpu.make_async_copy(
                    refs[q].at[pl.ds(16 * e, 16)], outs[e].at[:, at, :], sem.at[2 * q + e]
                )
            )
    for copy in copies:
        copy.start()
    for copy in copies:
        copy.wait()


def collect(tab, pieces):
    return call(
        collect_body,
        [jax.ShapeDtypeStruct((16, B, B), BF)] * 2,
        [SMEM] + [HBM] * 8,
        [pltpu.SemaphoreType.DMA((16,))],
    )(tab, *pieces)


def load(refs, groups, inv_s, low_s, inv_sem, low_sem):
    copies = []
    for g in range(groups):
        copies.append(
            pltpu.make_async_copy(refs[8 + g], low_s.at[pl.ds(16 * g, 16)], low_sem.at[g])
        )
    for q in range(8):
        for d in range(2):
            for h in range(2):
                n = 4 * q + 2 * d + h
                copies.append(
                    pltpu.make_async_copy(
                        refs[q].at[d, :, pl.ds(h * B, B)], inv_s.at[n], inv_sem.at[n]
                    )
                )
    for copy in copies:
        copy.start()
    return copies


def product(tab, inv_s, low_s, first, n):
    total = dot(inv_s[tab[POS_AT + first + n]], low_s[n])
    for j in range(1, 4):
        total += dot(inv_s[tab[POS_AT + first + n + j]], low_s[n + j])
    return total


def level_one_body(group, tab, *refs):
    rows_ref = refs[9]
    if group == 0:
        ups, diag_out = refs[10:12]
        inv_s, low_s, acc, diag, inv_sem, low_sem = refs[12:]
    else:
        first_ups, ups, diag_out, up_spread = refs[10:14]
        inv_s, low_s, acc, diag, inv_sem, low_sem = refs[14:]
    copies = load(refs, 1, inv_s, low_s, inv_sem, low_sem)
    acc[...] = jnp.zeros_like(acc)
    diag[...] = jnp.zeros_like(diag)
    for copy in copies:
        copy.wait()

    def step(n, carry):
        acc[...] += product(tab, inv_s, low_s, 16 * group, 4 * n)
        return carry

    lax.fori_loop(0, 4, step, 0)
    for i in range(2):
        rows = pl.ds(i * B, B)
        ups[rows, :] = jnp.zeros((B, B), BF)

        @pl.when(tab[ROW_AT + 4 * group + 2 * tab[CORE_AT] + i] > 0)
        def _():
            up = (-acc[rows, :]).astype(BF)
            ups[rows, :] = up
            diag[...] += dot_t(rows_ref[rows, :], up)

    if group == 1:
        for j in range(16):
            up_spread[j, 0] = first_ups[j * 32 : j * 32 + 32, :]
            up_spread[j, 1] = ups[j * 32 : j * 32 + 32, :]
    for k in range(8):
        at = pl.ds(pl.multiple_of(tab[SLICE_AT + k] * 32, 32), 32)
        diag_out[k] = diag[at, :]


def level_one(group, tab, pieces, low, rows, first_ups=None):
    shapes = [jax.ShapeDtypeStruct((HALF, B), BF), jax.ShapeDtypeStruct((8, 32, B), F32)]
    more = []
    if group == 1:
        shapes.append(jax.ShapeDtypeStruct((16, 2, 32, B), BF))
        more = [first_ups]

    def body(tab_ref, *refs):
        level_one_body(group, tab_ref, *refs)

    return call(
        body,
        shapes,
        [SMEM] + [HBM] * 9 + [VMEM] * (1 + len(more)),
        [
            pltpu.VMEM((32, HALF, B), BF),
            pltpu.VMEM((16, B, B), BF),
            pltpu.VMEM((HALF, B), F32),
            pltpu.VMEM((B, B), F32),
            pltpu.SemaphoreType.DMA((32,)),
            pltpu.SemaphoreType.DMA((1,)),
        ],
        limit=30,
        flops=2 * HALF * 16 * B * B,
        moved=12 * 2**20,
    )(tab, *pieces, low, rows, *more)


def kids_body(tab, *refs):
    part_own, part_sib, inv_s, low_s, inv_sem, low_sem = refs[10:]
    copies = load(refs, 2, inv_s, low_s, inv_sem, low_sem)
    part_own[...] = jnp.zeros_like(part_own)
    part_sib[...] = jnp.zeros_like(part_sib)
    for copy in copies:
        copy.wait()

    for g, part in enumerate((part_own, part_sib)):

        def step(n, carry):
            cols = pl.ds(pl.multiple_of((n // 2) * B, B), B)
            part[:, cols] += product(tab, inv_s, low_s.at[pl.ds(16 * g, 16)], 32 + 16 * g, 4 * n)
            return carry

        lax.fori_loop(0, 4, step, 0)


def kids(tab, pieces):
    return call(
        kids_body,
        [jax.ShapeDtypeStruct((HALF, 2 * B), F32)] * 2,
        [SMEM] + [HBM] * 10,
        [
            pltpu.VMEM((32, HALF, B), BF),
            pltpu.VMEM((32, B, B), BF),
            pltpu.SemaphoreType.DMA((32,)),
            pltpu.SemaphoreType.DMA((2,)),
        ],
        limit=56,
        flops=2 * LOC * 16 * B * B,
        moved=16 * 2**20,
    )(tab, *pieces)


def pack_body(parent, spread, dinv, *refs):
    terms, out, diag = refs[:8], refs[8], refs[9]
    total = terms[0][...]
    for i in range(1, 8):
        total = total + terms[i][...]
    value = dinv[...] - total
    diag[...] = value
    half = value.astype(BF)
    for j in range(16):
        for e in range(2):
            home = parent[2 * j + e]
            even, odd = (home // 2) * 2, home % 2
            out[j, e * 64 : e * 64 + 32, :] = spread[even, odd]
            out[j, e * 64 + 32 : e * 64 + 64, :] = spread[even + 1, 1 - odd]
        out[j, 128:160, :] = half


def level_zero_body(tab, got, part_own, part_sib, factor, link, up_ref, sums, both):
    both[...] = jnp.zeros_like(both)
    for e in range(2):
        cols = pl.ds(e * B, B)
        for rb in range(4):
            rows = pl.ds(rb * B, B)
            part_rows = pl.ds((rb % 2) * B, B)
            present = tab[ROW_AT + 4 * (e + 2) + rb] > 0

            @pl.when(jnp.logical_not(present))
            def _():
                up_ref[rows, cols] = jnp.zeros((B, B), BF)

            @pl.when(present)
            def _():
                start, at = 8 * (rb % 2), e * 64 + 32 * (rb // 2)
                above = got[start : start + 8, at : at + 32, :].reshape(B, B)
                part = jnp.where(
                    tab[CORE_AT] == rb // 2, part_own[part_rows, cols], part_sib[part_rows, cols]
                )
                low = factor[rows, cols]
                total = part + dot(above, link[:, cols])
                up = (-total).astype(BF)
                up_ref[rows, cols] = up
                both[0, :, cols] += dot_t(above, low)
                both[1, :, cols] += dot_t(low, up)

    for i in range(8):
        sums[i, 0:32, :] = both[0, i * 32 : i * 32 + 32, :]
        sums[i, 32:64, :] = both[1, i * 32 : i * 32 + 32, :]


def parent_body(tab, sums, got, link, diag, out):
    total = sums[0]
    for i in range(1, 8):
        total = total + sums[i]
    ups = []
    for e in range(2):
        cols = slice(e * B, e * B + B)
        half = got[tab[PAR_AT + e], 128:160, :]
        ups.append((-(total[0:32, cols] + dot(half, link[:, cols]))).astype(BF))
    up = jnp.concatenate(ups, axis=1)
    high = total[32:64].astype(BF)
    rest = (total[32:64] - high.astype(F32)).astype(BF)
    one_high = diag[...].astype(BF)
    one_rest = (diag[...] - one_high.astype(F32)).astype(BF)
    one = jnp.concatenate([one_high, one_rest], axis=1)
    for i in range(8):
        out[i, 96:128, :] = one
        out[i, 0:32, :] = up
        out[i, 32:64, :] = high
        out[i, 64:96, :] = rest


def last_body(got, dinv, link, up_ref, diag_ref, one_ref):
    for i in range(8):
        rows = pl.ds(i * 32, 32)
        up_ref[rows, :] = got[i, 0:32, :]
        one_ref[rows, :] = got[i, 96:128, 0:B].astype(F32) + got[i, 96:128, B : 2 * B].astype(F32)
        diag_ref[rows, :] = dinv[rows, :] - (
            got[i, 32:64, :].astype(F32) + got[i, 64:96, :].astype(F32)
        )
    for e in range(2):
        cols = pl.ds(e * B, B)
        diag_ref[:, cols] -= dot_t(link[:, cols], up_ref[:, cols])


def shards(
    inverse_anc,
    factor_one,
    factor_zero,
    factor_parent,
    dinv_one,
    dinv_zero,
    struct_one,
    select_zero,
    parent,
):
    row = lax.axis_index("prow")
    col = lax.axis_index("pcol")
    tab = pl.pallas_call(
        table_body,
        out_shape=jax.ShapeDtypeStruct((TABLE,), jnp.int32),
        in_specs=[SMEM] * 4,
        out_specs=SMEM,
    )(jnp.stack([row, col]).astype(jnp.int32), struct_one, select_zero, parent)
    link = lax.dynamic_slice_in_dim(factor_parent, col * 2 * B, 2 * B, 1)
    dinv_rows = lax.dynamic_slice_in_dim(dinv_one, row * 32, 32, 0)

    barrier = lax.optimization_barrier
    core = col % 2
    keep, give = core * HALF, (1 - core) * HALF
    spread_low = call(
        build_body, jax.ShapeDtypeStruct((8, 3, 4, 32, B), BF), [VMEM, VMEM]
    )(factor_one, factor_zero)
    spread_low = lax.all_to_all(spread_low, "prow", 0, 0)

    own_rows = lax.dynamic_slice_in_dim(factor_one, keep, HALF, 0)
    sib_rows = send(lax.dynamic_slice_in_dim(factor_one, give, HALF, 0), SIBLING)
    own = jnp.stack(
        [
            lax.dynamic_slice_in_dim(inverse_anc, keep, HALF, 0),
            send(lax.dynamic_slice_in_dim(inverse_anc, give, HALF, 0), SIBLING),
        ]
    )
    own, tab = barrier((own, tab))
    below, above = send(own, Z_UP), send(own, Z_DOWN)
    other = send(own, X_HI)
    own, spread_low, below, above, sib_rows = barrier((own, spread_low, below, above, sib_rows))
    far = send(below, Z_UP)
    mine = call(pick_body, jax.ShapeDtypeStruct((32, 32, B), BF), [SMEM, VMEM])(
        tab, spread_low.reshape(96, 32, B)
    )
    low_below, low_above = send(mine, Y_UP), send(mine, Y_DOWN)
    low_other = send(mine, X_LO)
    low_far = send(low_below, Y_UP)
    low_other_above = send(low_other, Y_DOWN)
    low_other_below = send(low_other, Y_UP)
    low_other_far = send(low_other_above, Y_DOWN)
    other_above, other_below = send(other, Z_DOWN), send(other, Z_UP)
    other_far = send(far, X_HI)
    low_pieces = [mine, low_above, low_far, low_below]
    low_pieces += [low_other, low_other_above, low_other_far, low_other_below]
    low_one, low_zero = collect(tab, low_pieces)
    low_one, low_zero, other_above, other_below, other_far = barrier(
        (low_one, low_zero, other_above, other_below, other_far)
    )
    low_one_sib = send(low_one, SIBLING)
    pieces = [own, above, far, below, other, other_above, other_far, other_below]

    up_own, diag_own = level_one(0, tab, pieces, low_one, own_rows)
    up_sib, diag_sib, up_spread = level_one(1, tab, pieces, low_one_sib, sib_rows, up_own)
    spread = lax.all_to_all(up_spread, "pcol", 0, 0)
    low_zero, up_spread2 = barrier((low_zero, up_spread))
    low_zero_sib = send(low_zero, SIBLING)
    diag_parts = diag_own + send(diag_sib, SIBLING)
    terms = [diag_parts[0]]
    for k in range(1, 8):
        terms.append(send(diag_parts[k], moves(dy=k % 4, dxl=k // 4)))
    part_own, part_sib = kids(tab, pieces + [low_zero, low_zero_sib])
    part_sib = send(part_sib, SIBLING)
    up_sib = send(up_sib, SIBLING)
    upper_one = jnp.zeros((LOC, B), BF)
    upper_one = lax.dynamic_update_slice_in_dim(upper_one, up_own, keep, 0)
    upper_one = lax.dynamic_update_slice_in_dim(upper_one, up_sib, give, 0)
    packed, diag_rows = call(
        pack_body,
        [jax.ShapeDtypeStruct((16, 160, B), BF), jax.ShapeDtypeStruct((32, B), F32)],
        [SMEM] + [VMEM] * 10,
    )(parent, spread, dinv_rows, *terms)
    got = lax.all_to_all(packed, "pcol", 0, 0)
    upper_zero, sums = call(
        level_zero_body,
        [jax.ShapeDtypeStruct((LOC, 2 * B), BF), jax.ShapeDtypeStruct((8, 64, 2 * B), F32)],
        [SMEM] + [VMEM] * 5,
        [pltpu.VMEM((2, B, 2 * B), F32)],
    )(tab, got, part_own, part_sib, factor_zero, link)
    sums = lax.all_to_all(sums, "prow", 0, 0)
    rows_out = call(
        parent_body,
        jax.ShapeDtypeStruct((8, 128, 2 * B), BF),
        [SMEM, VMEM, VMEM, VMEM, VMEM],
    )(tab, sums, got, link, diag_rows)
    rows_in = lax.all_to_all(rows_out, "prow", 0, 0)
    upper_parent, diag_zero, diag_one = call(
        last_body,
        [
            jax.ShapeDtypeStruct((B, 2 * B), BF),
            jax.ShapeDtypeStruct((B, 2 * B), F32),
            jax.ShapeDtypeStruct((B, B), F32),
        ],
        [VMEM, VMEM, VMEM],
    )(rows_in, dinv_zero, link)
    return upper_one, diag_one, upper_zero, upper_parent, diag_zero


def solution(mesh):
    in_specs = (
        P("prow", "pcol"),
        P("prow", "pcol"),
        P("prow", "pcol"),
        P(),
        P(None, "pcol"),
        P(None, "pcol"),
        P(),
        P(),
        P(),
    )
    out_specs = (
        P("prow", "pcol"),
        P(None, "pcol"),
        P("prow", "pcol"),
        P(None, "pcol"),
        P(None, "pcol"),
    )
    return jax.shard_map(shards, mesh=mesh, in_specs=in_specs, out_specs=out_specs, check_vma=False)
```

```python
import jax
import jax.numpy as jnp
from jax import lax
from jax.experimental import pallas as pl
from jax.experimental.pallas import tpu as pltpu
from jax.sharding import PartitionSpec as P

MESH_AXES = ("prow", "pcol")
BF = jnp.bfloat16
F32 = jnp.float32
B = 256
LOC = 1024
def moves(dy=0, dxl=0, dz=0, dxh=0, dcore=0):
    pairs = []
    for y in range(4):
        for xl in range(2):
            for z in range(4):
                for xh in range(2):
                    for core in range(2):
                        src = (y * 2 + xl) * 16 + z * 4 + xh * 2 + core
                        dst = (((y + dy) % 4) * 2 + (xl ^ dxl)) * 16
                        dst += ((z + dz) % 4) * 4 + (xh ^ dxh) * 2 + (core ^ dcore)
                        pairs.append((src, dst))
    return pairs


X_HI = moves(dxh=1)
X_LO = moves(dxl=1)
Z_UP = moves(dz=1)
Z_DOWN = moves(dz=-1)
Y_UP = moves(dy=1)
Y_DOWN = moves(dy=-1)
SIBLING = moves(dcore=1)


def send(block, pairs):
    return lax.ppermute(block, MESH_AXES, pairs)


def dot(left, right):
    return jnp.dot(left, right, preferred_element_type=F32)


def dot_t(left, right):
    return lax.dot_general(left, right, (((0,), (0,)), ((), ())), preferred_element_type=F32)


VMEM = pl.BlockSpec(memory_space=pltpu.VMEM)
SMEM = pl.BlockSpec(memory_space=pltpu.SMEM)
HBM = pl.BlockSpec(memory_space=pltpu.HBM)


def call(body, out_shape, in_specs, scratch=(), limit=32, flops=0, moved=0):
    outs = [VMEM] * len(out_shape) if isinstance(out_shape, list) else VMEM
    cost = pl.CostEstimate(flops=flops, bytes_accessed=moved, transcendentals=0)
    return pl.pallas_call(
        body,
        cost_estimate=cost if flops else None,
        out_shape=out_shape,
        in_specs=in_specs,
        out_specs=outs,
        scratch_shapes=list(scratch),
        compiler_params=pltpu.CompilerParams(vmem_limit_bytes=limit * 2**20),
    )


POS_AT = 0
SLICE_AT = 64
ROW_AT = 72
PAR_AT = 88
PICK_AT = 90
CORE_AT = 122
TABLE = 123
LISTS = ((0, 16), (16, 32), (32, 40), (40, 48), (48, 56), (56, 64))


def table_body(place, struct, select, parent, tab):
    row, col = place[0], place[1]
    core = col & 1
    y, xl = row >> 1, row & 1
    sib = col ^ 1
    blocks = [struct[col, n] for n in range(16)] + [struct[sib, n] for n in range(16)]
    for where in (col, sib):
        for e in range(2):
            kid = 2 * where + e
            home = parent[kid]
            blocks += [struct[home, select[kid, n]] for n in range(8)]
    for e in range(2):
        tab[PAR_AT + e] = parent[2 * col + e]
    for n, block in enumerate(blocks):
        home = block >> 1
        apart = ((home >> 2) - (col >> 2)) & 3
        other = (home ^ col) & 3
        tab[POS_AT + n] = 4 * apart + 16 * (other >> 1) + 2 * (other & 1) + (block & 1)
    for n in range(32):
        index = n if n < 16 else n + 16
        group = 0 if n < 16 else (1 if n < 24 else 2)
        block = blocks[index]
        tab[PICK_AT + n] = (block >> 2) * 12 + group * 4 + (block & 3)
    for n in range(ROW_AT, ROW_AT + 16):
        tab[n] = 0
    for group in range(4):
        low, high = LISTS[group]
        for n in range(low, high):
            block = blocks[n]

            @pl.when((block >> 2) == row)
            def _():
                tab[ROW_AT + 4 * group + (block & 3)] = 1

    for k in range(8):
        tab[SLICE_AT + k] = ((y + k) & 3) * 2 + (xl ^ (k // 4))
    tab[CORE_AT] = core


def build_body(one, zero, out):
    for i in range(8):
        for t in range(4):
            rows = pl.ds(t * B + i * 32, 32)
            out[i, 0, t] = one[rows, :]
            out[i, 1, t] = zero[rows, 0:B]
            out[i, 2, t] = zero[rows, B : 2 * B]


def pick_body(tab, spread, out):
    for n in range(32):
        out[n] = spread[tab[PICK_AT + n]]


HALF = LOC // 2


def collect_body(tab, *refs):
    outs, sem = refs[8:10], refs[10]
    copies = []
    for q in range(8):
        at = pl.ds(pl.multiple_of(tab[SLICE_AT + q] * 32, 32), 32)
        for e in range(2):
            copies.append(
                pltpu.make_async_copy(
                    refs[q].at[pl.ds(16 * e, 16)], outs[e].at[:, at, :], sem.at[2 * q + e]
                )
            )
    for copy in copies:
        copy.start()
    for copy in copies:
        copy.wait()


def collect(tab, pieces):
    return call(
        collect_body,
        [jax.ShapeDtypeStruct((16, B, B), BF)] * 2,
        [SMEM] + [HBM] * 8,
        [pltpu.SemaphoreType.DMA((16,))],
    )(tab, *pieces)


def load(refs, groups, inv_s, low_s, inv_sem, low_sem):
    copies = []
    for g in range(groups):
        copies.append(
            pltpu.make_async_copy(refs[8 + g], low_s.at[pl.ds(16 * g, 16)], low_sem.at[g])
        )
    for q in range(8):
        for d in range(2):
            for h in range(2):
                n = 4 * q + 2 * d + h
                copies.append(
                    pltpu.make_async_copy(
                        refs[q].at[d, :, pl.ds(h * B, B)], inv_s.at[n], inv_sem.at[n]
                    )
                )
    for copy in copies:
        copy.start()
    return copies


def product(tab, inv_s, low_s, first, n):
    total = dot(inv_s[tab[POS_AT + first + n]], low_s[n])
    for j in range(1, 4):
        total += dot(inv_s[tab[POS_AT + first + n + j]], low_s[n + j])
    return total


def level_one_body(group, tab, *refs):
    rows_ref = refs[9]
    if group == 0:
        ups, near, away = refs[10:13]
        inv_s, low_s, acc, diag, inv_sem, low_sem = refs[13:]
    else:
        first_ups, ups, near, away, up_spread = refs[10:15]
        inv_s, low_s, acc, diag, inv_sem, low_sem = refs[15:]
    copies = load(refs, 1, inv_s, low_s, inv_sem, low_sem)
    acc[...] = jnp.zeros_like(acc)
    diag[...] = jnp.zeros_like(diag)
    for copy in copies:
        copy.wait()

    def step(n, carry):
        acc[...] += product(tab, inv_s, low_s, 16 * group, 4 * n)
        return carry

    lax.fori_loop(0, 4, step, 0)
    for i in range(2):
        rows = pl.ds(i * B, B)
        ups[rows, :] = jnp.zeros((B, B), BF)

        @pl.when(tab[ROW_AT + 4 * group + 2 * tab[CORE_AT] + i] > 0)
        def _():
            up = (-acc[rows, :]).astype(BF)
            ups[rows, :] = up
            diag[...] += dot_t(rows_ref[rows, :], up)

    if group == 1:
        for j in range(16):
            up_spread[j, 0] = first_ups[j * 32 : j * 32 + 32, :]
            up_spread[j, 1] = ups[j * 32 : j * 32 + 32, :]
    for k in range(8):
        at = pl.ds(pl.multiple_of(tab[SLICE_AT + k] * 32, 32), 32)
        (near if k < 4 else away)[k % 4] = diag[at, :]


def level_one(group, tab, pieces, low, rows, first_ups=None):
    shapes = [jax.ShapeDtypeStruct((HALF, B), BF)]
    shapes += [jax.ShapeDtypeStruct((4, 32, B), F32)] * 2
    more = []
    if group == 1:
        shapes.append(jax.ShapeDtypeStruct((16, 2, 32, B), BF))
        more = [first_ups]

    def body(tab_ref, *refs):
        level_one_body(group, tab_ref, *refs)

    return call(
        body,
        shapes,
        [SMEM] + [HBM] * 9 + [VMEM] * (1 + len(more)),
        [
            pltpu.VMEM((32, HALF, B), BF),
            pltpu.VMEM((16, B, B), BF),
            pltpu.VMEM((HALF, B), F32),
            pltpu.VMEM((B, B), F32),
            pltpu.SemaphoreType.DMA((32,)),
            pltpu.SemaphoreType.DMA((1,)),
        ],
        limit=30,
        flops=2 * HALF * 16 * B * B,
        moved=12 * 2**20,
    )(tab, *pieces, low, rows, *more)


def kids_body(tab, *refs):
    part_own, part_sib, inv_s, low_s, inv_sem, low_sem = refs[10:]
    copies = load(refs, 2, inv_s, low_s, inv_sem, low_sem)
    part_own[...] = jnp.zeros_like(part_own)
    part_sib[...] = jnp.zeros_like(part_sib)
    for copy in copies:
        copy.wait()

    for g, part in enumerate((part_own, part_sib)):

        def step(n, carry):
            cols = pl.ds(pl.multiple_of((n // 2) * B, B), B)
            part[:, cols] += product(tab, inv_s, low_s.at[pl.ds(16 * g, 16)], 32 + 16 * g, 4 * n)
            return carry

        lax.fori_loop(0, 4, step, 0)


def kids(tab, pieces):
    return call(
        kids_body,
        [jax.ShapeDtypeStruct((HALF, 2 * B), F32)] * 2,
        [SMEM] + [HBM] * 10,
        [
            pltpu.VMEM((32, HALF, B), BF),
            pltpu.VMEM((32, B, B), BF),
            pltpu.SemaphoreType.DMA((32,)),
            pltpu.SemaphoreType.DMA((2,)),
        ],
        limit=56,
        flops=2 * LOC * 16 * B * B,
        moved=16 * 2**20,
    )(tab, *pieces)


def pack_body(parent, spread, dinv, *refs):
    terms, out, diag = refs[:4], refs[4], refs[5]
    total = terms[0][...]
    for i in range(1, 4):
        total = total + terms[i][...]
    value = dinv[...] - total
    diag[...] = value
    half = value.astype(BF)
    for j in range(16):
        for e in range(2):
            home = parent[2 * j + e]
            even, odd = (home // 2) * 2, home % 2
            out[j, e * 64 : e * 64 + 32, :] = spread[even, odd]
            out[j, e * 64 + 32 : e * 64 + 64, :] = spread[even + 1, 1 - odd]
        out[j, 128:160, :] = half


def level_zero_body(tab, got, part_own, part_sib, factor, link, up_ref, sums, both):
    both[...] = jnp.zeros_like(both)
    for e in range(2):
        cols = pl.ds(e * B, B)
        for rb in range(4):
            rows = pl.ds(rb * B, B)
            part_rows = pl.ds((rb % 2) * B, B)
            present = tab[ROW_AT + 4 * (e + 2) + rb] > 0

            @pl.when(jnp.logical_not(present))
            def _():
                up_ref[rows, cols] = jnp.zeros((B, B), BF)

            @pl.when(present)
            def _():
                start, at = 8 * (rb % 2), e * 64 + 32 * (rb // 2)
                above = got[start : start + 8, at : at + 32, :].reshape(B, B)
                part = jnp.where(
                    tab[CORE_AT] == rb // 2, part_own[part_rows, cols], part_sib[part_rows, cols]
                )
                low = factor[rows, cols]
                total = part + dot(above, link[:, cols])
                up = (-total).astype(BF)
                up_ref[rows, cols] = up
                both[0, :, cols] += dot_t(above, low)
                both[1, :, cols] += dot_t(low, up)

    for i in range(8):
        sums[i, 0:32, :] = both[0, i * 32 : i * 32 + 32, :]
        sums[i, 32:64, :] = both[1, i * 32 : i * 32 + 32, :]


def parent_body(tab, sums, got, link, diag, out):
    total = sums[0]
    for i in range(1, 8):
        total = total + sums[i]
    ups = []
    for e in range(2):
        cols = slice(e * B, e * B + B)
        half = got[tab[PAR_AT + e], 128:160, :]
        ups.append((-(total[0:32, cols] + dot(half, link[:, cols]))).astype(BF))
    up = jnp.concatenate(ups, axis=1)
    high = total[32:64].astype(BF)
    rest = (total[32:64] - high.astype(F32)).astype(BF)
    one_high = diag[...].astype(BF)
    one_rest = (diag[...] - one_high.astype(F32)).astype(BF)
    one = jnp.concatenate([one_high, one_rest], axis=1)
    for i in range(8):
        out[i, 96:128, :] = one
        out[i, 0:32, :] = up
        out[i, 32:64, :] = high
        out[i, 64:96, :] = rest


def last_body(got, dinv, link, up_ref, diag_ref, one_ref):
    for i in range(8):
        rows = pl.ds(i * 32, 32)
        up_ref[rows, :] = got[i, 0:32, :]
        one_ref[rows, :] = got[i, 96:128, 0:B].astype(F32) + got[i, 96:128, B : 2 * B].astype(F32)
        diag_ref[rows, :] = dinv[rows, :] - (
            got[i, 32:64, :].astype(F32) + got[i, 64:96, :].astype(F32)
        )
    for e in range(2):
        cols = pl.ds(e * B, B)
        diag_ref[:, cols] -= dot_t(link[:, cols], up_ref[:, cols])


def shards(
    inverse_anc,
    factor_one,
    factor_zero,
    factor_parent,
    dinv_one,
    dinv_zero,
    struct_one,
    select_zero,
    parent,
):
    row = lax.axis_index("prow")
    col = lax.axis_index("pcol")
    tab = pl.pallas_call(
        table_body,
        out_shape=jax.ShapeDtypeStruct((TABLE,), jnp.int32),
        in_specs=[SMEM] * 4,
        out_specs=SMEM,
    )(jnp.stack([row, col]).astype(jnp.int32), struct_one, select_zero, parent)
    link = lax.dynamic_slice_in_dim(factor_parent, col * 2 * B, 2 * B, 1)
    dinv_rows = lax.dynamic_slice_in_dim(dinv_one, row * 32, 32, 0)

    barrier = lax.optimization_barrier
    core = col % 2
    keep, give = core * HALF, (1 - core) * HALF
    spread_low = call(
        build_body, jax.ShapeDtypeStruct((8, 3, 4, 32, B), BF), [VMEM, VMEM]
    )(factor_one, factor_zero)
    spread_low = lax.all_to_all(spread_low, "prow", 0, 0)

    own_rows = lax.dynamic_slice_in_dim(factor_one, keep, HALF, 0)
    sib_rows = send(lax.dynamic_slice_in_dim(factor_one, give, HALF, 0), SIBLING)
    own = jnp.stack(
        [
            lax.dynamic_slice_in_dim(inverse_anc, keep, HALF, 0),
            send(lax.dynamic_slice_in_dim(inverse_anc, give, HALF, 0), SIBLING),
        ]
    )
    own, tab = barrier((own, tab))
    below, above = send(own, Z_UP), send(own, Z_DOWN)
    other = send(own, X_HI)
    own, spread_low, below, above, sib_rows = barrier((own, spread_low, below, above, sib_rows))
    far = send(below, Z_UP)
    mine = call(pick_body, jax.ShapeDtypeStruct((32, 32, B), BF), [SMEM, VMEM])(
        tab, spread_low.reshape(96, 32, B)
    )
    low_below, low_above = send(mine, Y_UP), send(mine, Y_DOWN)
    low_other = send(mine, X_LO)
    low_far = send(low_below, Y_UP)
    low_other_above = send(low_other, Y_DOWN)
    low_other_below = send(low_other, Y_UP)
    low_other_far = send(low_other_above, Y_DOWN)
    other_above, other_below = send(other, Z_DOWN), send(other, Z_UP)
    other_far = send(far, X_HI)
    low_pieces = [mine, low_above, low_far, low_below]
    low_pieces += [low_other, low_other_above, low_other_far, low_other_below]
    low_one, low_zero = collect(tab, low_pieces)
    low_one, low_zero, other_above, other_below, other_far = barrier(
        (low_one, low_zero, other_above, other_below, other_far)
    )
    low_one_sib = send(low_one, SIBLING)
    pieces = [own, above, far, below, other, other_above, other_far, other_below]

    up_own, near_own, away_own = level_one(0, tab, pieces, low_one, own_rows)
    up_sib, near_sib, away_sib, up_spread = level_one(1, tab, pieces, low_one_sib, sib_rows, up_own)
    spread = lax.all_to_all(up_spread, "pcol", 0, 0)
    low_zero, up_spread2 = barrier((low_zero, up_spread))
    low_zero_sib = send(low_zero, SIBLING)
    near = near_own + send(near_sib, SIBLING)
    near = near + send(away_own, X_LO) + send(away_sib, moves(dxl=1, dcore=1))
    terms = [near[0]]
    for k in range(1, 4):
        terms.append(send(near[k], moves(dy=k)))
    part_own, part_sib = kids(tab, pieces + [low_zero, low_zero_sib])
    part_sib = send(part_sib, SIBLING)
    up_sib, part_sib = lax.optimization_barrier((send(up_sib, SIBLING), part_sib))
    upper_one = jnp.zeros((LOC, B), BF)
    upper_one = lax.dynamic_update_slice_in_dim(upper_one, up_own, keep, 0)
    upper_one = lax.dynamic_update_slice_in_dim(upper_one, up_sib, give, 0)
    packed, diag_rows = call(
        pack_body,
        [jax.ShapeDtypeStruct((16, 160, B), BF), jax.ShapeDtypeStruct((32, B), F32)],
        [SMEM] + [VMEM] * 6,
    )(parent, spread, dinv_rows, *terms)
    got = lax.all_to_all(packed, "pcol", 0, 0)
    upper_zero, sums = call(
        level_zero_body,
        [jax.ShapeDtypeStruct((LOC, 2 * B), BF), jax.ShapeDtypeStruct((8, 64, 2 * B), F32)],
        [SMEM] + [VMEM] * 5,
        [pltpu.VMEM((2, B, 2 * B), F32)],
    )(tab, got, part_own, part_sib, factor_zero, link)
    sums = lax.all_to_all(sums, "prow", 0, 0)
    rows_out = call(
        parent_body,
        jax.ShapeDtypeStruct((8, 128, 2 * B), BF),
        [SMEM, VMEM, VMEM, VMEM, VMEM],
    )(tab, sums, got, link, diag_rows)
    rows_in = lax.all_to_all(rows_out, "prow", 0, 0)
    upper_parent, diag_zero, diag_one = call(
        last_body,
        [
            jax.ShapeDtypeStruct((B, 2 * B), BF),
            jax.ShapeDtypeStruct((B, 2 * B), F32),
            jax.ShapeDtypeStruct((B, B), F32),
        ],
        [VMEM, VMEM, VMEM],
    )(rows_in, dinv_zero, link)
    return upper_one, diag_one, upper_zero, upper_parent, diag_zero


def solution(mesh):
    in_specs = (
        P("prow", "pcol"),
        P("prow", "pcol"),
        P("prow", "pcol"),
        P(),
        P(None, "pcol"),
        P(None, "pcol"),
        P(),
        P(),
        P(),
    )
    out_specs = (
        P("prow", "pcol"),
        P(None, "pcol"),
        P("prow", "pcol"),
        P(None, "pcol"),
        P(None, "pcol"),
    )
    return jax.shard_map(shards, mesh=mesh, in_specs=in_specs, out_specs=out_specs, check_vma=False)
```

```python
import jax
import jax.numpy as jnp
from jax import lax
from jax.experimental import pallas as pl
from jax.experimental.pallas import tpu as pltpu
from jax.sharding import PartitionSpec as P

MESH_AXES = ("prow", "pcol")
BF = jnp.bfloat16
F32 = jnp.float32
B = 256
LOC = 1024
def moves(dy=0, dxl=0, dz=0, dxh=0, dcore=0):
    pairs = []
    for y in range(4):
        for xl in range(2):
            for z in range(4):
                for xh in range(2):
                    for core in range(2):
                        src = (y * 2 + xl) * 16 + z * 4 + xh * 2 + core
                        dst = (((y + dy) % 4) * 2 + (xl ^ dxl)) * 16
                        dst += ((z + dz) % 4) * 4 + (xh ^ dxh) * 2 + (core ^ dcore)
                        pairs.append((src, dst))
    return pairs


X_HI = moves(dxh=1)
X_LO = moves(dxl=1)
Z_UP = moves(dz=1)
Z_DOWN = moves(dz=-1)
Y_UP = moves(dy=1)
Y_DOWN = moves(dy=-1)
SIBLING = moves(dcore=1)


def send(block, pairs):
    return lax.ppermute(block, MESH_AXES, pairs)


def dot(left, right):
    return jnp.dot(left, right, preferred_element_type=F32)


def dot_t(left, right):
    return lax.dot_general(left, right, (((0,), (0,)), ((), ())), preferred_element_type=F32)


VMEM = pl.BlockSpec(memory_space=pltpu.VMEM)
SMEM = pl.BlockSpec(memory_space=pltpu.SMEM)
HBM = pl.BlockSpec(memory_space=pltpu.HBM)


def call(body, out_shape, in_specs, scratch=(), limit=16, flops=0, moved=0):
    outs = [VMEM] * len(out_shape) if isinstance(out_shape, list) else VMEM
    cost = pl.CostEstimate(flops=flops, bytes_accessed=moved, transcendentals=0)
    return pl.pallas_call(
        body,
        cost_estimate=cost if flops else None,
        out_shape=out_shape,
        in_specs=in_specs,
        out_specs=outs,
        scratch_shapes=list(scratch),
        compiler_params=pltpu.CompilerParams(vmem_limit_bytes=limit * 2**20),
    )


POS_AT = 0
SLICE_AT = 64
ROW_AT = 72
PAR_AT = 88
PICK_AT = 90
CORE_AT = 122
TABLE = 123
LISTS = ((0, 16), (16, 32), (32, 40), (40, 48), (48, 56), (56, 64))


def table_body(place, struct, select, parent, tab):
    row, col = place[0], place[1]
    core = col & 1
    y, xl = row >> 1, row & 1
    sib = col ^ 1
    blocks = [struct[col, n] for n in range(16)] + [struct[sib, n] for n in range(16)]
    for where in (col, sib):
        for e in range(2):
            kid = 2 * where + e
            home = parent[kid]
            blocks += [struct[home, select[kid, n]] for n in range(8)]
    for e in range(2):
        tab[PAR_AT + e] = parent[2 * col + e]
    for n, block in enumerate(blocks):
        home = block >> 1
        apart = ((home >> 2) - (col >> 2)) & 3
        other = (home ^ col) & 3
        tab[POS_AT + n] = 4 * apart + 16 * (other >> 1) + 2 * (other & 1) + (block & 1)
    for n in range(32):
        index = n if n < 16 else n + 16
        group = 0 if n < 16 else (1 if n < 24 else 2)
        block = blocks[index]
        tab[PICK_AT + n] = (block >> 2) * 12 + group * 4 + (block & 3)
    for n in range(ROW_AT, ROW_AT + 16):
        tab[n] = 0
    for group in range(4):
        low, high = LISTS[group]
        for n in range(low, high):
            block = blocks[n]

            @pl.when((block >> 2) == row)
            def _():
                tab[ROW_AT + 4 * group + (block & 3)] = 1

    for k in range(8):
        tab[SLICE_AT + k] = ((y + k) & 3) * 2 + (xl ^ (k // 4))
    tab[CORE_AT] = core


def build_body(one, zero, out):
    for i in range(8):
        for t in range(4):
            rows = pl.ds(t * B + i * 32, 32)
            out[i, 0, t] = one[rows, :]
            out[i, 1, t] = zero[rows, 0:B]
            out[i, 2, t] = zero[rows, B : 2 * B]


def pick_body(tab, spread, out):
    for n in range(32):
        out[n] = spread[tab[PICK_AT + n]]


HALF = LOC // 2


def collect_body(tab, *refs):
    outs, sem = refs[8:10], refs[10]
    copies = []
    for q in range(8):
        at = pl.ds(pl.multiple_of(tab[SLICE_AT + q] * 32, 32), 32)
        for e in range(2):
            copies.append(
                pltpu.make_async_copy(
                    refs[q].at[pl.ds(16 * e, 16)], outs[e].at[:, at, :], sem.at[2 * q + e]
                )
            )
    for copy in copies:
        copy.start()
    for copy in copies:
        copy.wait()


def collect(tab, pieces):
    return call(
        collect_body,
        [jax.ShapeDtypeStruct((16, B, B), BF)] * 2,
        [SMEM] + [HBM] * 8,
        [pltpu.SemaphoreType.DMA((16,))],
    )(tab, *pieces)


def load(refs, groups, inv_s, low_s, inv_sem, low_sem):
    copies = []
    for g in range(groups):
        copies.append(
            pltpu.make_async_copy(refs[8 + g], low_s.at[pl.ds(16 * g, 16)], low_sem.at[g])
        )
    for q in range(8):
        for d in range(2):
            for h in range(2):
                n = 4 * q + 2 * d + h
                copies.append(
                    pltpu.make_async_copy(
                        refs[q].at[d, :, pl.ds(h * B, B)], inv_s.at[n], inv_sem.at[n]
                    )
                )
    for copy in copies:
        copy.start()
    return copies


def product(tab, inv_s, low_s, first, n):
    total = dot(inv_s[tab[POS_AT + first + n]], low_s[n])
    for j in range(1, 4):
        total += dot(inv_s[tab[POS_AT + first + n + j]], low_s[n + j])
    return total


def level_one_body(group, tab, *refs):
    rows_ref = refs[9]
    if group == 0:
        ups, near, away = refs[10:13]
        inv_s, low_s, acc, diag, inv_sem, low_sem = refs[13:]
    else:
        first_ups, ups, near, away, up_spread = refs[10:15]
        inv_s, low_s, acc, diag, inv_sem, low_sem = refs[15:]
    copies = load(refs, 1, inv_s, low_s, inv_sem, low_sem)
    acc[...] = jnp.zeros_like(acc)
    diag[...] = jnp.zeros_like(diag)
    for copy in copies:
        copy.wait()

    def step(n, carry):
        acc[...] += product(tab, inv_s, low_s, 16 * group, 4 * n)
        return carry

    lax.fori_loop(0, 4, step, 0)
    for i in range(2):
        rows = pl.ds(i * B, B)
        ups[rows, :] = jnp.zeros((B, B), BF)

        @pl.when(tab[ROW_AT + 4 * group + 2 * tab[CORE_AT] + i] > 0)
        def _():
            up = (-acc[rows, :]).astype(BF)
            ups[rows, :] = up
            diag[...] += dot_t(rows_ref[rows, :], up)

    if group == 1:
        for j in range(16):
            up_spread[j, 0] = first_ups[j * 32 : j * 32 + 32, :]
            up_spread[j, 1] = ups[j * 32 : j * 32 + 32, :]
    for k in range(8):
        at = pl.ds(pl.multiple_of(tab[SLICE_AT + k] * 32, 32), 32)
        (near if k < 4 else away)[k % 4] = diag[at, :]


def level_one(group, tab, pieces, low, rows, first_ups=None):
    shapes = [jax.ShapeDtypeStruct((HALF, B), BF)]
    shapes += [jax.ShapeDtypeStruct((4, 32, B), F32)] * 2
    more = []
    if group == 1:
        shapes.append(jax.ShapeDtypeStruct((16, 2, 32, B), BF))
        more = [first_ups]

    def body(tab_ref, *refs):
        level_one_body(group, tab_ref, *refs)

    return call(
        body,
        shapes,
        [SMEM] + [HBM] * 9 + [VMEM] * (1 + len(more)),
        [
            pltpu.VMEM((32, HALF, B), BF),
            pltpu.VMEM((16, B, B), BF),
            pltpu.VMEM((HALF, B), F32),
            pltpu.VMEM((B, B), F32),
            pltpu.SemaphoreType.DMA((32,)),
            pltpu.SemaphoreType.DMA((1,)),
        ],
        limit=30,
        flops=2 * HALF * 16 * B * B,
        moved=12 * 2**20,
    )(tab, *pieces, low, rows, *more)


def kids_body(tab, *refs):
    part_own, part_sib, inv_s, low_s, inv_sem, low_sem = refs[10:]
    copies = load(refs, 2, inv_s, low_s, inv_sem, low_sem)
    part_own[...] = jnp.zeros_like(part_own)
    part_sib[...] = jnp.zeros_like(part_sib)
    for copy in copies:
        copy.wait()

    for g, part in enumerate((part_own, part_sib)):

        def step(n, carry):
            cols = pl.ds(pl.multiple_of((n // 2) * B, B), B)
            part[:, cols] += product(tab, inv_s, low_s.at[pl.ds(16 * g, 16)], 32 + 16 * g, 4 * n)
            return carry

        lax.fori_loop(0, 4, step, 0)


def kids(tab, pieces):
    return call(
        kids_body,
        [jax.ShapeDtypeStruct((HALF, 2 * B), F32)] * 2,
        [SMEM] + [HBM] * 10,
        [
            pltpu.VMEM((32, HALF, B), BF),
            pltpu.VMEM((32, B, B), BF),
            pltpu.SemaphoreType.DMA((32,)),
            pltpu.SemaphoreType.DMA((2,)),
        ],
        limit=56,
        flops=2 * LOC * 16 * B * B,
        moved=16 * 2**20,
    )(tab, *pieces)


def pack_body(parent, spread, dinv, *refs):
    terms, out, diag = refs[:4], refs[4], refs[5]
    total = terms[0][...]
    for i in range(1, 4):
        total = total + terms[i][...]
    value = dinv[...] - total
    diag[...] = value
    half = value.astype(BF)
    for j in range(16):
        for e in range(2):
            home = parent[2 * j + e]
            even, odd = (home // 2) * 2, home % 2
            out[j, e * 64 : e * 64 + 32, :] = spread[even, odd]
            out[j, e * 64 + 32 : e * 64 + 64, :] = spread[even + 1, 1 - odd]
        out[j, 128:160, :] = half


def level_zero_body(tab, got, part_own, part_sib, factor, link, up_ref, sums, both):
    both[...] = jnp.zeros_like(both)
    for e in range(2):
        cols = pl.ds(e * B, B)
        for rb in range(4):
            rows = pl.ds(rb * B, B)
            part_rows = pl.ds((rb % 2) * B, B)
            present = tab[ROW_AT + 4 * (e + 2) + rb] > 0

            @pl.when(jnp.logical_not(present))
            def _():
                up_ref[rows, cols] = jnp.zeros((B, B), BF)

            @pl.when(present)
            def _():
                start, at = 8 * (rb % 2), e * 64 + 32 * (rb // 2)
                above = got[start : start + 8, at : at + 32, :].reshape(B, B)
                part = jnp.where(
                    tab[CORE_AT] == rb // 2, part_own[part_rows, cols], part_sib[part_rows, cols]
                )
                low = factor[rows, cols]
                total = part + dot(above, link[:, cols])
                up = (-total).astype(BF)
                up_ref[rows, cols] = up
                both[0, :, cols] += dot_t(above, low)
                both[1, :, cols] += dot_t(low, up)

    for i in range(8):
        sums[i, 0:32, :] = both[0, i * 32 : i * 32 + 32, :]
        sums[i, 32:64, :] = both[1, i * 32 : i * 32 + 32, :]


def parent_body(tab, sums, got, link, diag, out):
    total = sums[0]
    for i in range(1, 8):
        total = total + sums[i]
    ups = []
    for e in range(2):
        cols = slice(e * B, e * B + B)
        half = got[tab[PAR_AT + e], 128:160, :]
        ups.append((-(total[0:32, cols] + dot(half, link[:, cols]))).astype(BF))
    up = jnp.concatenate(ups, axis=1)
    high = total[32:64].astype(BF)
    rest = (total[32:64] - high.astype(F32)).astype(BF)
    one_high = diag[...].astype(BF)
    one_rest = (diag[...] - one_high.astype(F32)).astype(BF)
    one = jnp.concatenate([one_high, one_rest], axis=1)
    for i in range(8):
        out[i, 96:128, :] = one
        out[i, 0:32, :] = up
        out[i, 32:64, :] = high
        out[i, 64:96, :] = rest


def last_body(got, dinv, link, up_ref, diag_ref, one_ref):
    for i in range(8):
        rows = pl.ds(i * 32, 32)
        up_ref[rows, :] = got[i, 0:32, :]
        one_ref[rows, :] = got[i, 96:128, 0:B].astype(F32) + got[i, 96:128, B : 2 * B].astype(F32)
        diag_ref[rows, :] = dinv[rows, :] - (
            got[i, 32:64, :].astype(F32) + got[i, 64:96, :].astype(F32)
        )
    for e in range(2):
        cols = pl.ds(e * B, B)
        diag_ref[:, cols] -= dot_t(link[:, cols], up_ref[:, cols])


def shards(
    inverse_anc,
    factor_one,
    factor_zero,
    factor_parent,
    dinv_one,
    dinv_zero,
    struct_one,
    select_zero,
    parent,
):
    row = lax.axis_index("prow")
    col = lax.axis_index("pcol")
    tab = pl.pallas_call(
        table_body,
        out_shape=jax.ShapeDtypeStruct((TABLE,), jnp.int32),
        in_specs=[SMEM] * 4,
        out_specs=SMEM,
    )(jnp.stack([row, col]).astype(jnp.int32), struct_one, select_zero, parent)
    link = lax.dynamic_slice_in_dim(factor_parent, col * 2 * B, 2 * B, 1)
    dinv_rows = lax.dynamic_slice_in_dim(dinv_one, row * 32, 32, 0)

    barrier = lax.optimization_barrier
    core = col % 2
    keep, give = core * HALF, (1 - core) * HALF
    spread_low = call(
        build_body, jax.ShapeDtypeStruct((8, 3, 4, 32, B), BF), [VMEM, VMEM]
    )(factor_one, factor_zero)
    spread_low = lax.all_to_all(spread_low, "prow", 0, 0)

    own_rows = lax.dynamic_slice_in_dim(factor_one, keep, HALF, 0)
    sib_rows = send(lax.dynamic_slice_in_dim(factor_one, give, HALF, 0), SIBLING)
    own = jnp.stack(
        [
            lax.dynamic_slice_in_dim(inverse_anc, keep, HALF, 0),
            send(lax.dynamic_slice_in_dim(inverse_anc, give, HALF, 0), SIBLING),
        ]
    )
    own, tab = barrier((own, tab))
    below, above = send(own, Z_UP), send(own, Z_DOWN)
    other = send(own, X_HI)
    own, spread_low, below, above, sib_rows = barrier((own, spread_low, below, above, sib_rows))
    far = send(below, Z_UP)
    mine = call(pick_body, jax.ShapeDtypeStruct((32, 32, B), BF), [SMEM, VMEM])(
        tab, spread_low.reshape(96, 32, B)
    )
    low_below, low_above = send(mine, Y_UP), send(mine, Y_DOWN)
    low_other = send(mine, X_LO)
    low_far = send(low_below, Y_UP)
    low_other_above = send(low_other, Y_DOWN)
    low_other_below = send(low_other, Y_UP)
    low_other_far = send(low_other_above, Y_DOWN)
    other_above, other_below = send(other, Z_DOWN), send(other, Z_UP)
    other_far = send(far, X_HI)
    low_pieces = [mine, low_above, low_far, low_below]
    low_pieces += [low_other, low_other_above, low_other_far, low_other_below]
    low_one, low_zero = collect(tab, low_pieces)
    low_one, low_zero, other_above, other_below, other_far = barrier(
        (low_one, low_zero, other_above, other_below, other_far)
    )
    low_one_sib = send(low_one, SIBLING)
    pieces = [own, above, far, below, other, other_above, other_far, other_below]

    up_own, near_own, away_own = level_one(0, tab, pieces, low_one, own_rows)
    up_sib, near_sib, away_sib, up_spread = level_one(1, tab, pieces, low_one_sib, sib_rows, up_own)
    spread = lax.all_to_all(up_spread, "pcol", 0, 0)
    low_zero, up_spread2 = barrier((low_zero, up_spread))
    low_zero_sib = send(low_zero, SIBLING)
    near = near_own + send(near_sib, SIBLING)
    near = near + send(away_own, X_LO) + send(away_sib, moves(dxl=1, dcore=1))
    terms = [near[0]]
    for k in range(1, 4):
        terms.append(send(near[k], moves(dy=k)))
    part_own, part_sib = kids(tab, pieces + [low_zero, low_zero_sib])
    part_sib = send(part_sib, SIBLING)
    up_sib, part_sib = lax.optimization_barrier((send(up_sib, SIBLING), part_sib))
    upper_one = jnp.zeros((LOC, B), BF)
    upper_one = lax.dynamic_update_slice_in_dim(upper_one, up_own, keep, 0)
    upper_one = lax.dynamic_update_slice_in_dim(upper_one, up_sib, give, 0)
    packed, diag_rows = call(
        pack_body,
        [jax.ShapeDtypeStruct((16, 160, B), BF), jax.ShapeDtypeStruct((32, B), F32)],
        [SMEM] + [VMEM] * 6,
    )(parent, spread, dinv_rows, *terms)
    got = lax.all_to_all(packed, "pcol", 0, 0)
    upper_zero, sums = call(
        level_zero_body,
        [jax.ShapeDtypeStruct((LOC, 2 * B), BF), jax.ShapeDtypeStruct((8, 64, 2 * B), F32)],
        [SMEM] + [VMEM] * 5,
        [pltpu.VMEM((2, B, 2 * B), F32)],
    )(tab, got, part_own, part_sib, factor_zero, link)
    sums = lax.all_to_all(sums, "prow", 0, 0)
    rows_out = call(
        parent_body,
        jax.ShapeDtypeStruct((8, 128, 2 * B), BF),
        [SMEM, VMEM, VMEM, VMEM, VMEM],
    )(tab, sums, got, link, diag_rows)
    rows_in = lax.all_to_all(rows_out, "prow", 0, 0)
    upper_parent, diag_zero, diag_one = call(
        last_body,
        [
            jax.ShapeDtypeStruct((B, 2 * B), BF),
            jax.ShapeDtypeStruct((B, 2 * B), F32),
            jax.ShapeDtypeStruct((B, B), F32),
        ],
        [VMEM, VMEM, VMEM],
    )(rows_in, dinv_zero, link)
    return upper_one, diag_one, upper_zero, upper_parent, diag_zero


def solution(mesh):
    in_specs = (
        P("prow", "pcol"),
        P("prow", "pcol"),
        P("prow", "pcol"),
        P(),
        P(None, "pcol"),
        P(None, "pcol"),
        P(),
        P(),
        P(),
    )
    out_specs = (
        P("prow", "pcol"),
        P(None, "pcol"),
        P("prow", "pcol"),
        P(None, "pcol"),
        P(None, "pcol"),
    )
    return jax.shard_map(shards, mesh=mesh, in_specs=in_specs, out_specs=out_specs, check_vma=False)
```
